32 devices in a mesh: groups: 2 (over x), tm: 16 (over z, y, core).
Axes of the slice: x: 2, y: 2, z: 4, core: 2. Of those that a mesh axis runs over, the one named last changes fastest.
Arguments:
- start_state: float32 [6, 96, 96], P('groups'), parts along dimension 0, may hold values from -0.9 to 0.9
- mobility: float32 [16, 192, 96], P('tm', 'groups'), parts along dimension 1, may hold values from 0.5 to 2
Outputs:
- final_state: float32 [16, 6, 96, 96], P('tm', 'groups'), parts along dimension 1
The draws below stay inside these ranges and needn't reach their ends.
There are 2 independent parts, one for each index of `groups`. The reference program is written for one: setup_inputs(seed, part) draws one part's arguments, and reference() takes and returns one part's arrays. A program takes and returns all parts, laid end to end along the dimension named above; each array names one. Nothing has to cross between parts.
All inputs are finite; a program needn't handle non-finite values.
Results may differ from the reference program's by a relative error of at most 0.00029.
Values sent between devices are 32-bit elements; how exact they have to be, the bound alone decides.
A program may use at most 128 MiB of HBM per device.

```python
import math
import jax
import jax.numpy as jnp
from jax import lax

G = 96
ITERS = 2
SLICES = 16
N_TM = 16


def level_of(key, dims, pieces, smallest, high):
    level, own = 1.0, jax.random.fold_in(key, 6)
    for dim, shards_of in pieces:
        steps = jnp.exp(jax.random.uniform(jax.random.fold_in(own, dim), (shards_of,), jnp.float32, smallest / len(pieces), high / len(pieces)))
        level = level * jnp.repeat(steps, dims[dim] // shards_of).reshape([-1 if axis == dim else 1 for axis in range(len(dims))])
    return level


def setup_inputs(seed: int = 0, part: int = 0) -> dict:
    keys = jax.random.split(jax.random.key(seed), 3)
    own_keys = jax.random.split(jax.random.fold_in(keys[2], part), 3)
    return {
        "start_state": jnp.clip(jax.random.uniform(own_keys[0], (3, G, G), jnp.float32, -0.9, 0.9), -0.9, 0.9),
        "mobility": jnp.clip(jnp.exp(math.log(2.0) - 1.3862944 * jax.random.uniform(own_keys[1], (SLICES, G, G), jnp.float32) ** level_of(own_keys[1], (SLICES, G, G), ((0, 16),), -0.2, 0.2)), 0.5, 2.0),
    }


time_step = 0.015
kappa_coef = 1.0
coupling = 0.5
strain_diffusion = 0.5
relax_rate = 2.0
misfit_one = 0.6
misfit_two = -0.4
mean_mobility = 1.0


def laplace(field):
    return (jnp.roll(field, 1, -2) + jnp.roll(field, -1, -2) + jnp.roll(field, 1, -1)
            + jnp.roll(field, -1, -1) - 4.0 * field)


def fine_rate(state, face_x, face_y):
    concentration = state[..., 0, :, :]
    strain_one = state[..., 1, :, :]
    strain_two = state[..., 2, :, :]
    potential = (concentration * concentration * concentration - concentration
                 - kappa_coef * laplace(concentration) + coupling * (strain_one + strain_two))
    flux_x = face_x * (jnp.roll(potential, -1, -2) - potential)
    flux_y = face_y * (jnp.roll(potential, -1, -1) - potential)
    rate_conc = flux_x - jnp.roll(flux_x, 1, -2) + flux_y - jnp.roll(flux_y, 1, -1)
    rate_one = strain_diffusion * laplace(strain_one) - relax_rate * (strain_one - misfit_one * concentration)
    rate_two = strain_diffusion * laplace(strain_two) - relax_rate * (strain_two - misfit_two * concentration)
    return jnp.stack([rate_conc, rate_one, rate_two], axis=-3)


def coarse_rate(state):
    concentration = state[..., 0, :, :]
    strain_one = state[..., 1, :, :]
    strain_two = state[..., 2, :, :]
    potential = -concentration - kappa_coef * 0.25 * laplace(concentration) + coupling * (strain_one + strain_two)
    rate_conc = mean_mobility * 0.25 * laplace(potential)
    rate_one = strain_diffusion * 0.25 * laplace(strain_one) - relax_rate * (strain_one - misfit_one * concentration)
    rate_two = strain_diffusion * 0.25 * laplace(strain_two) - relax_rate * (strain_two - misfit_two * concentration)
    return jnp.stack([rate_conc, rate_one, rate_two], axis=-3)


def restrict(field):
    half = field.shape[-1] // 2
    blocks = field.reshape(field.shape[:-2] + (half, 2, half, 2))
    return blocks.mean(axis=(-3, -1))


def prolong(field):
    return jnp.repeat(jnp.repeat(field, 2, -2), 2, -1)


def reference(start_state, mobility):
    face_x = 0.5 * (mobility + jnp.roll(mobility, -1, -2))
    face_y = 0.5 * (mobility + jnp.roll(mobility, -1, -1))
    spread = jnp.broadcast_to(start_state, (N_TM,) + start_state.shape)
    initial_rate = fine_rate(spread, face_x, face_y)
    first = spread
    middle = spread
    rates = [initial_rate, initial_rate, initial_rate]
    coarse_start = restrict(start_state)
    last = spread
    for sweep_index in range(ITERS):
        rate_first = fine_rate(first, face_x, face_y)
        middle = (first + 0.5 * time_step * (rate_first - rates[0])
                  + time_step * (5.0 / 24.0 * rates[0] + 1.0 / 3.0 * rates[1] - 1.0 / 24.0 * rates[2]))
        rate_middle = fine_rate(middle, face_x, face_y)
        swept = (middle + 0.5 * time_step * (rate_middle - rates[1])
                 + time_step * (-1.0 / 24.0 * rates[0] + 1.0 / 3.0 * rates[1] + 5.0 / 24.0 * rates[2]))
        rate_last = fine_rate(swept, face_x, face_y)
        integral = time_step * (rate_first / 6.0 + 2.0 / 3.0 * rate_middle + rate_last / 6.0)
        coarse_first = restrict(first)
        offsets = restrict(integral) - time_step * coarse_rate(coarse_first)

        def advance(carry, offset):
            following = carry + time_step * coarse_rate(carry) + offset
            return following, carry

        unused, coarse_begin = lax.scan(advance, coarse_start, offsets)
        coarse_end = coarse_begin + time_step * coarse_rate(coarse_begin) + offsets
        begin_shift = coarse_begin - coarse_first
        end_shift = coarse_end - restrict(swept)
        middle = middle + prolong(0.5 * (begin_shift + end_shift))
        last = swept + prolong(end_shift)
        if sweep_index + 1 < ITERS:
            received = jnp.concatenate([start_state[None], swept[:-1]], axis=0)
            first = received + prolong(coarse_begin - restrict(received))
            rates = [rate_first, fine_rate(middle, face_x, face_y), fine_rate(last, face_x, face_y)]
    return last
```

```python
import functools

import jax
import jax.numpy as jnp
import ml_dtypes
import numpy as np
from jax import lax
from jax.experimental import pallas as pl
from jax.experimental.pallas import tpu as pltpu
from jax.sharding import PartitionSpec as P

DT = 0.015
KAPPA = 1.0
ETA = 0.5
DE = 0.5
GAMMA = 2.0
M1 = 0.6
M2 = -0.4
MEAN = 1.0
LANES = 128
ROWS = 8
PER = 1
F32 = jnp.float32
BF16 = jnp.bfloat16


def split(matrix):
    high = matrix.astype(ml_dtypes.bfloat16)
    low = (matrix - high.astype(np.float64)).astype(ml_dtypes.bfloat16)
    return high, low


def constants(grid):
    half = grid // 2
    tiles = half // 4
    rows = tiles * ROWS
    wave = np.arange(half)
    angle = 2.0 * np.pi * np.outer(wave, wave) / half
    basis = (np.cos(angle) + np.sin(angle)) / np.sqrt(half)
    mean = 0.5 * np.repeat(basis, 2, axis=1)
    spread = np.repeat(basis, 2, axis=0)
    edge = (LANES - grid) // 2
    lane = np.arange(LANES)
    column = np.where(lane < grid, lane, np.where(lane < grid + edge, lane - grid, lane - 2 * edge))
    left = np.zeros((2 * rows, 3 * grid))
    right = np.zeros((2 * LANES, LANES))
    back_right = np.zeros((LANES, 2 * LANES))
    back_left = np.zeros((3 * grid, 2 * rows))
    square = np.sin(np.pi * wave / half) ** 2
    step = np.zeros((4, rows, LANES))
    for s in range(2):
        right[s * LANES : s * LANES + grid, s * half : (s + 1) * half] = mean.T
        back_right[s * half : (s + 1) * half, s * LANES : (s + 1) * LANES] = spread[column].T
        lanes = slice(s * half, (s + 1) * half)
        for j in range(tiles):
            for h in range(2):
                a = 4 * j + 2 * h + s
                sym = -(square[a] + square)
                for f in range(3):
                    row = ROWS * j + 2 * f + h
                    left[s * rows + row, f * grid : (f + 1) * grid] = mean[a]
                    back_left[f * grid : (f + 1) * grid, s * rows + row] = spread[:, a]
                row = ROWS * j + h
                step[0, row, lanes] = MEAN * (-sym - KAPPA * sym * sym)
                step[1, row, lanes] = MEAN * ETA * sym
                step[2, row, lanes] = MEAN * ETA * sym
                step[0, row + 2, lanes] = DE * sym - GAMMA
                step[0, row + 4, lanes] = DE * sym - GAMMA
                step[3, row + 2, lanes] = GAMMA * M1
                step[2, row + 4, lanes] = GAMMA * M2
    step = (DT * step).astype(np.float32).reshape(4, tiles, ROWS, LANES)
    pieces = []
    for matrix in (left, right, back_right, back_left):
        pieces.extend(split(matrix))
    return pieces + [step]


def product_left(pair, x):
    high_c, low_c = pair
    high = x.astype(BF16)
    low = (x - high.astype(F32)).astype(BF16)
    dot = functools.partial(jnp.dot, preferred_element_type=F32)
    return dot(high_c, high) + (dot(high_c, low) + dot(low_c, high))


def product_right(x, pair):
    high_c, low_c = pair
    high = x.astype(BF16)
    low = (x - high.astype(F32)).astype(BF16)
    dot = functools.partial(jnp.dot, preferred_element_type=F32)
    return dot(high, high_c) + (dot(low, high_c) + dot(high, low_c))


def up(x):
    return pltpu.roll(x, x.shape[0] - 1, 0)


def down(x):
    return pltpu.roll(x, 1, 0)


def west(x):
    return pltpu.roll(x, LANES - 1, 1)


def east(x):
    return pltpu.roll(x, 1, 1)


def laplace(x):
    return (up(x) + down(x)) + (west(x) + east(x)) - 4.0 * x


def fine_rate(state, face_x, face_y):
    c, one, two = state
    mu = c * c * c - c - KAPPA * laplace(c) + ETA * (one + two)
    jx = face_x * (up(mu) - mu)
    jy = face_y * (west(mu) - mu)
    rate_c = (jx - down(jx)) + (jy - east(jy))
    rate_one = DE * laplace(one) - GAMMA * (one - M1 * c)
    rate_two = DE * laplace(two) - GAMMA * (two - M2 * c)
    return rate_c, rate_one, rate_two


def combine(*terms):
    total = None
    for weight, state in terms:
        part = state if weight == 1.0 else tuple(weight * x for x in state)
        total = part if total is None else tuple(a + b for a, b in zip(total, part))
    return total


def block_mean(state):
    out = []
    for x in state:
        rows, lanes = x.shape
        lane = lax.broadcasted_iota(jnp.int32, x.shape, 1)
        row = lax.broadcasted_iota(jnp.int32, x.shape, 0)
        x = x + jnp.where(lane % 2 == 0, west(x), east(x))
        x = x + jnp.where(row % 2 == 0, up(x), down(x))
        out.append(0.25 * x)
    return tuple(out)


def mode_rate(step, modes):
    axis = modes.ndim - 2
    return (
        step[0] * modes
        + step[1] * pltpu.roll(modes, ROWS - 2, axis)
        + step[2] * pltpu.roll(modes, 4, axis)
        + step[3] * pltpu.roll(modes, 2, axis)
    )


def kernel(
    n, scanners,
    start_ref, mob_ref, lh, ll, rh, rl, brh, brl, blh, bll, step_ref,
    out_ref,
    wide, fluct, arrived, modes, gathered, results, returned,
    w_send, w_recv, send_one, recv_one, send_two, recv_two,
):
    me = lax.axis_index("tm")
    grid = mob_ref.shape[-1]
    edge = (LANES - grid) // 2
    tiles = step_ref.shape[1]
    count = len(scanners)
    per = tiles // count
    MESH = pl.DeviceIdType.MESH

    barrier = pltpu.get_barrier_semaphore()

    def greet(k, carry):
        other = lax.rem(me + k, n)
        pl.semaphore_signal(barrier, inc=1, device_id={"tm": other}, device_id_type=MESH)
        return carry

    lax.fori_loop(1, n, greet, 0)

    lane = lax.broadcasted_iota(jnp.int32, (grid, LANES), 1)

    def widen(x, slot):
        wide[slot, :, :grid] = x
        x = wide[slot]
        return jnp.where(
            lane < grid,
            x,
            jnp.where(lane < grid + edge, pltpu.roll(x, grid, 1), pltpu.roll(x, 2 * edge, 1)),
        )

    mob = widen(mob_ref[0], 3)
    face_x = 0.5 * (mob + up(mob))
    face_y = 0.5 * (mob + west(mob))
    rate = lambda state: fine_rate(state, face_x, face_y)

    def forward(state):
        x = jnp.concatenate(state, axis=0)
        rows = tiles * ROWS
        g = product_left((lh[...], ll[...]), x)
        g = jnp.concatenate([g[:rows], g[rows:]], axis=1)
        return product_right(g, (rh[...], rl[...])).reshape(tiles, ROWS, LANES)

    def inverse(parts):
        rows = tiles * ROWS
        x = jnp.concatenate([p.reshape(rows, LANES) for p in parts], axis=0)
        z = product_right(x, (brh[...], brl[...]))
        z = jnp.concatenate(
            [
                jnp.concatenate([z[k * rows : (k + 1) * rows, s * LANES : (s + 1) * LANES] for k in range(len(parts))], axis=1)
                for s in range(2)
            ],
            axis=0,
        )
        y = product_left((blh[...], bll[...]), z)
        return [
            tuple(y[f * grid : (f + 1) * grid, k * LANES : (k + 1) * LANES] for f in range(3))
            for k in range(len(parts))
        ]

    step = [step_ref[k] for k in range(4)]

    def remote(src, dst, send, recv, target):
        return pltpu.make_async_remote_copy(
            src_ref=src, dst_ref=dst, send_sem=send, recv_sem=recv,
            device_id={"tm": target}, device_id_type=MESH,
        )

    def drain(ref, sem):
        pltpu.make_async_copy(ref, ref, sem).wait()

    def is_scanner():
        hit = me == scanners[0]
        for d in scanners[1:]:
            hit = jnp.logical_or(hit, me == d)
        return hit

    def scan(it, start_modes_ref, offsets, inclusive):
        modes[it] = offsets
        for s, d in enumerate(scanners):
            @pl.when(me != d)
            def _():
                remote(
                    modes.at[it, pl.ds(s * per, per)], gathered.at[it, me],
                    send_one.at[it], recv_one.at[it], d,
                ).start()
        for s, d in enumerate(scanners):
            @pl.when(me == d)
            def _():
                mine = [step_ref[k, s * per : (s + 1) * per] for k in range(4)]
                state = start_modes_ref[s * per : (s + 1) * per]
                gathered[it, d] = modes[it, s * per : (s + 1) * per]
                drain(gathered.at[it, pl.ds(0, n - 1)], recv_one.at[it])
                for k in range(n):
                    after = None
                    if inclusive or k + 1 < n:
                        after = state + (mode_rate(mine, state) + gathered[it, k])
                    value = after if inclusive else state
                    results[it, k] = value
                    if k == d:
                        returned[it, s * per : (s + 1) * per] = value
                    else:
                        remote(
                            results.at[it, k], returned.at[it, pl.ds(s * per, per)],
                            send_two.at[it], recv_two.at[it], k,
                        ).start()
                    state = after

    def scanned(it):
        one_of = is_scanner()

        @pl.when(one_of)
        def _():
            drain(returned.at[it, pl.ds(0, (count - 1) * per)], recv_two.at[it])

        @pl.when(jnp.logical_not(one_of))
        def _():
            drain(returned.at[it], recv_two.at[it])

        return returned[it]

    u0 = tuple(widen(start_ref[f], f) for f in range(3))
    f0 = rate(u0)
    u1 = combine((1.0, u0), (0.5 * DT, f0))
    a1 = rate(u1)
    w = combine((1.0, u1), (0.5 * DT, a1))
    pw = block_mean(w)
    wf = combine((1.0, w), (-1.0, pw))
    for f in range(3):
        fluct[f] = wf[f]
    start_modes = forward(u0)
    modes[2] = start_modes
    pl.semaphore_wait(barrier, n - 1)

    @pl.when(me + 1 < n)
    def _():
        remote(fluct, arrived, w_send, w_recv, me + 1).start()

    a2 = rate(w)
    integral = combine((DT / 6.0, f0), (DT * 2.0 / 3.0, a1), (DT / 6.0, a2))
    offsets = forward(integral) - mode_rate(step, start_modes)
    scan(0, modes.at[2], offsets, False)

    p0 = block_mean(u0)
    u1f = combine((1.0, u1), (-0.5, p0), (-0.5, pw))

    @pl.when(me == 0)
    def _():
        for f in range(3):
            arrived[f] = u0[f] - p0[f]

    begin = scanned(0)
    end = begin + (mode_rate(step, begin) + offsets)
    pb, pe = inverse([begin, end])

    @pl.when(me > 0)
    def _():
        drain(arrived, w_recv)

    u0 = tuple(arrived[f] + pb[f] for f in range(3))
    u1 = combine((1.0, u1f), (0.5, pb), (0.5, pe))
    u2 = combine((1.0, wf), (1.0, pe))
    f1 = rate(u1)
    f2 = rate(u2)
    a0 = rate(u0)
    u1 = combine(
        (1.0, u0), (0.5 * DT, a0), (DT * (5.0 / 24.0 - 0.5), f0), (DT / 3.0, f1), (-DT / 24.0, f2)
    )
    a1 = rate(u1)
    w = combine(
        (1.0, u1), (0.5 * DT, a1), (-DT / 24.0, f0), (DT * (1.0 / 3.0 - 0.5), f1), (DT * 5.0 / 24.0, f2)
    )
    a2 = rate(w)
    integral = combine((DT / 6.0, a0), (DT * 2.0 / 3.0, a1), (DT / 6.0, a2))
    offsets = forward(integral) - mode_rate(step, begin)
    scan(1, modes.at[2], offsets, True)
    pw = block_mean(w)
    wf = combine((1.0, w), (-1.0, pw))
    for f in range(3):
        wide[f] = wf[f]
    (pe,) = inverse([scanned(1)])
    for f in range(3):
        out_ref[0, f] = (wide[f] + pe[f])[:, :grid]

    @pl.when(me + 1 < n)
    def _():
        drain(fluct, w_send)

    one_of = is_scanner()
    for it in range(2):
        @pl.when(one_of)
        def _():
            drain(modes.at[it, pl.ds(0, (count - 1) * per)], send_one.at[it])
            drain(results.at[it, pl.ds(0, n - 1)], send_two.at[it])

        @pl.when(jnp.logical_not(one_of))
        def _():
            drain(modes.at[it], send_one.at[it])


def local(n, start_state, mobility):
    grid = start_state.shape[-1]
    made = constants(grid)
    tiles = made[-1].shape[1]
    count = tiles // PER
    scanners = tuple(s * n // count for s in range(count))
    return pl.pallas_call(
        functools.partial(kernel, n, scanners),
        out_shape=jax.ShapeDtypeStruct((1,) + start_state.shape, F32),
        in_specs=[pl.BlockSpec(memory_space=pltpu.VMEM)] * (2 + len(made)),
        out_specs=pl.BlockSpec(memory_space=pltpu.VMEM),
        scratch_shapes=[
            pltpu.VMEM((4, grid, LANES), F32),
            pltpu.VMEM((3, grid, LANES), F32),
            pltpu.VMEM((3, grid, LANES), F32),
            pltpu.VMEM((3, tiles, ROWS, LANES), F32),
            pltpu.VMEM((2, n, PER, ROWS, LANES), F32),
            pltpu.VMEM((2, n, PER, ROWS, LANES), F32),
            pltpu.VMEM((2, tiles, ROWS, LANES), F32),
            pltpu.SemaphoreType.DMA,
            pltpu.SemaphoreType.DMA,
            pltpu.SemaphoreType.DMA((2,)),
            pltpu.SemaphoreType.DMA((2,)),
            pltpu.SemaphoreType.DMA((2,)),
            pltpu.SemaphoreType.DMA((2,)),
        ],
        compiler_params=pltpu.CompilerParams(
            collective_id=0, has_side_effects=True, vmem_limit_bytes=40 * 1024 * 1024
        ),
        cost_estimate=pl.CostEstimate(flops=200_000_000, bytes_accessed=1_500_000, transcendentals=0),
    )(start_state, mobility, *[jnp.asarray(m) for m in made])


def solution(mesh):
    n = mesh.shape["tm"]
    in_specs = (P("groups", None, None), P("tm", "groups", None))
    out_specs = P("tm", "groups", None, None)
    return jax.shard_map(
        functools.partial(local, n), mesh=mesh, in_specs=in_specs, out_specs=out_specs, check_vma=False
    )
```

```python
import functools

import jax
import jax.numpy as jnp
import ml_dtypes
import numpy as np
from jax import lax
from jax.experimental import pallas as pl
from jax.experimental.pallas import tpu as pltpu
from jax.sharding import PartitionSpec as P

DT = 0.015
KAPPA = 1.0
ETA = 0.5
DE = 0.5
GAMMA = 2.0
M1 = 0.6
M2 = -0.4
MEAN = 1.0
LANES = 128
ROWS = 8
PER = 1
F32 = jnp.float32
BF16 = jnp.bfloat16


def split(matrix):
    high = matrix.astype(ml_dtypes.bfloat16)
    low = (matrix - high.astype(np.float64)).astype(ml_dtypes.bfloat16)
    return high, low


def constants(grid):
    half = grid // 2
    tiles = half // 4
    rows = tiles * ROWS
    wave = np.arange(half)
    angle = 2.0 * np.pi * np.outer(wave, wave) / half
    basis = (np.cos(angle) + np.sin(angle)) / np.sqrt(half)
    mean = 0.5 * np.repeat(basis, 2, axis=1)
    spread = np.repeat(basis, 2, axis=0)
    edge = (LANES - grid) // 2
    lane = np.arange(LANES)
    column = np.where(lane < grid, lane, np.where(lane < grid + edge, lane - grid, lane - 2 * edge))
    left = np.zeros((2 * rows, 3 * grid))
    right = np.zeros((2 * LANES, LANES))
    back_right = np.zeros((LANES, 2 * LANES))
    back_left = np.zeros((3 * grid, 2 * rows))
    square = np.sin(np.pi * wave / half) ** 2
    step = np.zeros((4, rows, LANES))
    for s in range(2):
        right[s * LANES : s * LANES + grid, s * half : (s + 1) * half] = mean.T
        back_right[s * half : (s + 1) * half, s * LANES : (s + 1) * LANES] = spread[column].T
        lanes = slice(s * half, (s + 1) * half)
        for j in range(tiles):
            for h in range(2):
                a = 4 * j + 2 * h + s
                sym = -(square[a] + square)
                for f in range(3):
                    row = ROWS * j + 2 * f + h
                    left[s * rows + row, f * grid : (f + 1) * grid] = mean[a]
                    back_left[f * grid : (f + 1) * grid, s * rows + row] = spread[:, a]
                row = ROWS * j + h
                step[0, row, lanes] = MEAN * (-sym - KAPPA * sym * sym)
                step[1, row, lanes] = MEAN * ETA * sym
                step[2, row, lanes] = MEAN * ETA * sym
                step[0, row + 2, lanes] = DE * sym - GAMMA
                step[0, row + 4, lanes] = DE * sym - GAMMA
                step[3, row + 2, lanes] = GAMMA * M1
                step[2, row + 4, lanes] = GAMMA * M2
    step = (DT * step).astype(np.float32).reshape(4, tiles, ROWS, LANES)
    return [np.stack(split(matrix)) for matrix in (left, right, back_right, back_left)] + [step]


def product_left(pair, x):
    high_c, low_c = pair
    high = x.astype(BF16)
    low = (x - high.astype(F32)).astype(BF16)
    dot = functools.partial(jnp.dot, preferred_element_type=F32)
    return dot(high_c, high) + (dot(high_c, low) + dot(low_c, high))


def product_right(x, pair):
    high_c, low_c = pair
    high = x.astype(BF16)
    low = (x - high.astype(F32)).astype(BF16)
    dot = functools.partial(jnp.dot, preferred_element_type=F32)
    return dot(high, high_c) + (dot(low, high_c) + dot(high, low_c))


def up(x):
    return pltpu.roll(x, x.shape[0] - 1, 0)


def down(x):
    return pltpu.roll(x, 1, 0)


def west(x):
    return pltpu.roll(x, LANES - 1, 1)


def east(x):
    return pltpu.roll(x, 1, 1)


def laplace(x):
    return (up(x) + down(x)) + (west(x) + east(x)) - 4.0 * x


def fine_rate(state, face_x, face_y):
    c, one, two = state
    mu = c * c * c - c - KAPPA * laplace(c) + ETA * (one + two)
    jx = face_x * (up(mu) - mu)
    jy = face_y * (west(mu) - mu)
    rate_c = (jx - down(jx)) + (jy - east(jy))
    rate_one = DE * laplace(one) - GAMMA * (one - M1 * c)
    rate_two = DE * laplace(two) - GAMMA * (two - M2 * c)
    return rate_c, rate_one, rate_two


def combine(*terms):
    total = None
    for weight, state in terms:
        part = state if weight == 1.0 else tuple(weight * x for x in state)
        total = part if total is None else tuple(a + b for a, b in zip(total, part))
    return total


def block_mean(state):
    out = []
    for x in state:
        rows, lanes = x.shape
        lane = lax.broadcasted_iota(jnp.int32, x.shape, 1)
        row = lax.broadcasted_iota(jnp.int32, x.shape, 0)
        x = x + jnp.where(lane % 2 == 0, west(x), east(x))
        x = x + jnp.where(row % 2 == 0, up(x), down(x))
        out.append(0.25 * x)
    return tuple(out)


def mode_rate(step, modes):
    axis = modes.ndim - 2
    return (
        step[0] * modes
        + step[1] * pltpu.roll(modes, ROWS - 2, axis)
        + step[2] * pltpu.roll(modes, 4, axis)
        + step[3] * pltpu.roll(modes, 2, axis)
    )


def kernel(
    n, scanners,
    start_hbm, mob_hbm, left_hbm, right_hbm, back_right_hbm, back_left_hbm, step_hbm,
    out_ref,
    start_ref, mob_ref, left_ref, right_ref, back_right_ref, back_left_ref, step_ref, loaded,
    wide, fluct, arrived, modes, gathered, results, returned,
    w_send, w_recv, send_one, recv_one, send_two, recv_two,
):
    me = lax.axis_index("tm")
    grid = mob_ref.shape[-1]
    edge = (LANES - grid) // 2
    tiles = step_ref.shape[1]
    count = len(scanners)
    per = tiles // count
    MESH = pl.DeviceIdType.MESH

    loads = [
        pltpu.make_async_copy(src, dst, loaded.at[k])
        for k, (src, dst) in enumerate(
            [
                (start_hbm, start_ref),
                (mob_hbm, mob_ref),
                (left_hbm, left_ref),
                (right_hbm, right_ref),
                (step_hbm, step_ref),
                (back_right_hbm, back_right_ref),
                (back_left_hbm, back_left_ref),
            ]
        )
    ]
    for load in loads:
        load.start()
    barrier = pltpu.get_barrier_semaphore()

    def greet(k, carry):
        other = lax.rem(me + k, n)
        pl.semaphore_signal(barrier, inc=1, device_id={"tm": other}, device_id_type=MESH)
        return carry

    lax.fori_loop(1, n, greet, 0)

    lane = lax.broadcasted_iota(jnp.int32, (grid, LANES), 1)

    def widen(x, slot):
        wide[slot, :, :grid] = x
        x = wide[slot]
        return jnp.where(
            lane < grid,
            x,
            jnp.where(lane < grid + edge, pltpu.roll(x, grid, 1), pltpu.roll(x, 2 * edge, 1)),
        )

    loads[1].wait()
    mob = widen(mob_ref[0], 3)
    face_x = 0.5 * (mob + up(mob))
    face_y = 0.5 * (mob + west(mob))
    rate = lambda state: fine_rate(state, face_x, face_y)

    def forward(state):
        x = jnp.concatenate(state, axis=0)
        rows = tiles * ROWS
        g = product_left((left_ref[0], left_ref[1]), x)
        g = jnp.concatenate([g[:rows], g[rows:]], axis=1)
        return product_right(g, (right_ref[0], right_ref[1])).reshape(tiles, ROWS, LANES)

    def inverse(parts):
        rows = tiles * ROWS
        x = jnp.concatenate([p.reshape(rows, LANES) for p in parts], axis=0)
        z = product_right(x, (back_right_ref[0], back_right_ref[1]))
        z = jnp.concatenate(
            [
                jnp.concatenate([z[k * rows : (k + 1) * rows, s * LANES : (s + 1) * LANES] for k in range(len(parts))], axis=1)
                for s in range(2)
            ],
            axis=0,
        )
        y = product_left((back_left_ref[0], back_left_ref[1]), z)
        return [
            tuple(y[f * grid : (f + 1) * grid, k * LANES : (k + 1) * LANES] for f in range(3))
            for k in range(len(parts))
        ]

    def remote(src, dst, send, recv, target):
        return pltpu.make_async_remote_copy(
            src_ref=src, dst_ref=dst, send_sem=send, recv_sem=recv,
            device_id={"tm": target}, device_id_type=MESH,
        )

    def drain(ref, sem):
        pltpu.make_async_copy(ref, ref, sem).wait()

    def is_scanner():
        hit = me == scanners[0]
        for d in scanners[1:]:
            hit = jnp.logical_or(hit, me == d)
        return hit

    def scan(it, start_modes_ref, offsets, inclusive):
        modes[it] = offsets
        for s, d in enumerate(scanners):
            @pl.when(me != d)
            def _():
                remote(
                    modes.at[it, pl.ds(s * per, per)], gathered.at[it, me],
                    send_one.at[it], recv_one.at[it], d,
                ).start()
        for s, d in enumerate(scanners):
            @pl.when(me == d)
            def _():
                mine = [step_ref[k, s * per : (s + 1) * per] for k in range(4)]
                state = start_modes_ref[s * per : (s + 1) * per]
                gathered[it, d] = modes[it, s * per : (s + 1) * per]
                drain(gathered.at[it, pl.ds(0, n - 1)], recv_one.at[it])
                for k in range(n):
                    after = None
                    if inclusive or k + 1 < n:
                        after = state + (mode_rate(mine, state) + gathered[it, k])
                    value = after if inclusive else state
                    results[it, k] = value
                    if k == d:
                        returned[it, s * per : (s + 1) * per] = value
                    else:
                        remote(
                            results.at[it, k], returned.at[it, pl.ds(s * per, per)],
                            send_two.at[it], recv_two.at[it], k,
                        ).start()
                    state = after

    def scanned(it):
        one_of = is_scanner()

        @pl.when(one_of)
        def _():
            drain(returned.at[it, pl.ds(0, (count - 1) * per)], recv_two.at[it])

        @pl.when(jnp.logical_not(one_of))
        def _():
            drain(returned.at[it], recv_two.at[it])

        return returned[it]

    loads[0].wait()
    u0 = tuple(widen(start_ref[f], f) for f in range(3))
    f0 = rate(u0)
    u1 = combine((1.0, u0), (0.5 * DT, f0))
    a1 = rate(u1)
    w = combine((1.0, u1), (0.5 * DT, a1))
    pw = block_mean(w)
    wf = combine((1.0, w), (-1.0, pw))
    for f in range(3):
        fluct[f] = wf[f]
    for k in (2, 3, 4):
        loads[k].wait()
    step = [step_ref[k] for k in range(4)]
    start_modes = forward(u0)
    modes[2] = start_modes
    pl.semaphore_wait(barrier, n - 1)

    @pl.when(me + 1 < n)
    def _():
        remote(fluct, arrived, w_send, w_recv, me + 1).start()

    a2 = rate(w)
    integral = combine((DT / 6.0, f0), (DT * 2.0 / 3.0, a1), (DT / 6.0, a2))
    offsets = forward(integral) - mode_rate(step, start_modes)
    scan(0, modes.at[2], offsets, False)

    p0 = block_mean(u0)
    u1f = combine((1.0, u1), (-0.5, p0), (-0.5, pw))

    @pl.when(me == 0)
    def _():
        for f in range(3):
            arrived[f] = u0[f] - p0[f]

    for k in (5, 6):
        loads[k].wait()
    begin = scanned(0)
    end = begin + (mode_rate(step, begin) + offsets)
    pb, pe = inverse([begin, end])

    @pl.when(me > 0)
    def _():
        drain(arrived, w_recv)

    u0 = tuple(arrived[f] + pb[f] for f in range(3))
    u1 = combine((1.0, u1f), (0.5, pb), (0.5, pe))
    u2 = combine((1.0, wf), (1.0, pe))
    f1 = rate(u1)
    f2 = rate(u2)
    a0 = rate(u0)
    u1 = combine(
        (1.0, u0), (0.5 * DT, a0), (DT * (5.0 / 24.0 - 0.5), f0), (DT / 3.0, f1), (-DT / 24.0, f2)
    )
    a1 = rate(u1)
    w = combine(
        (1.0, u1), (0.5 * DT, a1), (-DT / 24.0, f0), (DT * (1.0 / 3.0 - 0.5), f1), (DT * 5.0 / 24.0, f2)
    )
    a2 = rate(w)
    integral = combine((DT / 6.0, a0), (DT * 2.0 / 3.0, a1), (DT / 6.0, a2))
    offsets = forward(integral) - mode_rate(step, begin)
    scan(1, modes.at[2], offsets, True)
    pw = block_mean(w)
    wf = combine((1.0, w), (-1.0, pw))
    for f in range(3):
        wide[f] = wf[f]
    (pe,) = inverse([scanned(1)])
    for f in range(3):
        out_ref[0, f] = (wide[f] + pe[f])[:, :grid]

    @pl.when(me + 1 < n)
    def _():
        drain(fluct, w_send)

    one_of = is_scanner()
    for it in range(2):
        @pl.when(one_of)
        def _():
            drain(modes.at[it, pl.ds(0, (count - 1) * per)], send_one.at[it])
            drain(results.at[it, pl.ds(0, n - 1)], send_two.at[it])

        @pl.when(jnp.logical_not(one_of))
        def _():
            drain(modes.at[it], send_one.at[it])


def local(n, start_state, mobility):
    grid = start_state.shape[-1]
    made = constants(grid)
    tiles = made[-1].shape[1]
    count = tiles // PER
    scanners = tuple(s * n // count for s in range(count))
    return pl.pallas_call(
        functools.partial(kernel, n, scanners),
        out_shape=jax.ShapeDtypeStruct((1,) + start_state.shape, F32),
        in_specs=[pl.BlockSpec(memory_space=pl.ANY)] * (2 + len(made)),
        out_specs=pl.BlockSpec(memory_space=pltpu.VMEM),
        scratch_shapes=[pltpu.VMEM(x.shape, x.dtype) for x in (start_state, mobility, *made)]
        + [
            pltpu.SemaphoreType.DMA((2 + len(made),)),
            pltpu.VMEM((4, grid, LANES), F32),
            pltpu.VMEM((3, grid, LANES), F32),
            pltpu.VMEM((3, grid, LANES), F32),
            pltpu.VMEM((3, tiles, ROWS, LANES), F32),
            pltpu.VMEM((2, n, PER, ROWS, LANES), F32),
            pltpu.VMEM((2, n, PER, ROWS, LANES), F32),
            pltpu.VMEM((2, tiles, ROWS, LANES), F32),
            pltpu.SemaphoreType.DMA,
            pltpu.SemaphoreType.DMA,
            pltpu.SemaphoreType.DMA((2,)),
            pltpu.SemaphoreType.DMA((2,)),
            pltpu.SemaphoreType.DMA((2,)),
            pltpu.SemaphoreType.DMA((2,)),
        ],
        compiler_params=pltpu.CompilerParams(
            collective_id=0, has_side_effects=True, vmem_limit_bytes=60 * 1024 * 1024
        ),
        cost_estimate=pl.CostEstimate(flops=200_000_000, bytes_accessed=1_500_000, transcendentals=0),
    )(start_state, mobility, *[jnp.asarray(m) for m in made])


def solution(mesh):
    n = mesh.shape["tm"]
    in_specs = (P("groups", None, None), P("tm", "groups", None))
    out_specs = P("tm", "groups", None, None)
    return jax.shard_map(
        functools.partial(local, n), mesh=mesh, in_specs=in_specs, out_specs=out_specs, check_vma=False
    )
```

```python
import functools

import jax
import jax.numpy as jnp
import ml_dtypes
import numpy as np
from jax import lax
from jax.experimental import pallas as pl
from jax.experimental.pallas import tpu as pltpu
from jax.sharding import PartitionSpec as P

DT = 0.015
KAPPA = 1.0
ETA = 0.5
DE = 0.5
GAMMA = 2.0
M1 = 0.6
M2 = -0.4
MEAN = 1.0
LANES = 128
ROWS = 8
PER = 2
F32 = jnp.float32
BF16 = jnp.bfloat16


def split(matrix):
    high = matrix.astype(ml_dtypes.bfloat16)
    low = (matrix - high.astype(np.float64)).astype(ml_dtypes.bfloat16)
    return high, low


def constants(grid):
    half = grid // 2
    tiles = half // 4
    rows = tiles * ROWS
    wave = np.arange(half)
    angle = 2.0 * np.pi * np.outer(wave, wave) / half
    basis = (np.cos(angle) + np.sin(angle)) / np.sqrt(half)
    mean = 0.5 * np.repeat(basis, 2, axis=1)
    spread = np.repeat(basis, 2, axis=0)
    edge = (LANES - grid) // 2
    lane = np.arange(LANES)
    column = np.where(lane < grid, lane, np.where(lane < grid + edge, lane - grid, lane - 2 * edge))
    left = np.zeros((2 * rows, 3 * grid))
    right = np.zeros((2 * LANES, LANES))
    back_right = np.zeros((LANES, 2 * LANES))
    back_left = np.zeros((3 * grid, 2 * rows))
    square = np.sin(np.pi * wave / half) ** 2
    step = np.zeros((4, rows, LANES))
    for s in range(2):
        right[s * LANES : s * LANES + grid, s * half : (s + 1) * half] = mean.T
        back_right[s * half : (s + 1) * half, s * LANES : (s + 1) * LANES] = spread[column].T
        lanes = slice(s * half, (s + 1) * half)
        for j in range(tiles):
            for h in range(2):
                a = 4 * j + 2 * h + s
                sym = -(square[a] + square)
                for f in range(3):
                    row = ROWS * j + 2 * f + h
                    left[s * rows + row, f * grid : (f + 1) * grid] = mean[a]
                    back_left[f * grid : (f + 1) * grid, s * rows + row] = spread[:, a]
                row = ROWS * j + h
                step[0, row, lanes] = MEAN * (-sym - KAPPA * sym * sym)
                step[1, row, lanes] = MEAN * ETA * sym
                step[2, row, lanes] = MEAN * ETA * sym
                step[0, row + 2, lanes] = DE * sym - GAMMA
                step[0, row + 4, lanes] = DE * sym - GAMMA
                step[3, row + 2, lanes] = GAMMA * M1
                step[2, row + 4, lanes] = GAMMA * M2
    step = (DT * step).astype(np.float32).reshape(4, tiles, ROWS, LANES)
    return [np.stack(split(matrix)) for matrix in (left, right, back_right, back_left)] + [step]


def product_left(pair, x):
    high_c, low_c = pair
    high = x.astype(BF16)
    low = (x - high.astype(F32)).astype(BF16)
    dot = functools.partial(jnp.dot, preferred_element_type=F32)
    return dot(high_c, high) + (dot(high_c, low) + dot(low_c, high))


def product_right(x, pair):
    high_c, low_c = pair
    high = x.astype(BF16)
    low = (x - high.astype(F32)).astype(BF16)
    dot = functools.partial(jnp.dot, preferred_element_type=F32)
    return dot(high, high_c) + (dot(low, high_c) + dot(high, low_c))


def up(x):
    return pltpu.roll(x, x.shape[0] - 1, 0)


def down(x):
    return pltpu.roll(x, 1, 0)


def west(x):
    return pltpu.roll(x, LANES - 1, 1)


def east(x):
    return pltpu.roll(x, 1, 1)


def laplace(x):
    return (up(x) + down(x)) + (west(x) + east(x)) - 4.0 * x


def fine_rate(state, face_x, face_y):
    c, one, two = state
    mu = c * c * c - c - KAPPA * laplace(c) + ETA * (one + two)
    jx = face_x * (up(mu) - mu)
    jy = face_y * (west(mu) - mu)
    rate_c = (jx - down(jx)) + (jy - east(jy))
    rate_one = DE * laplace(one) - GAMMA * (one - M1 * c)
    rate_two = DE * laplace(two) - GAMMA * (two - M2 * c)
    return rate_c, rate_one, rate_two


def combine(*terms):
    total = None
    for weight, state in terms:
        part = state if weight == 1.0 else tuple(weight * x for x in state)
        total = part if total is None else tuple(a + b for a, b in zip(total, part))
    return total


def block_mean(state):
    out = []
    for x in state:
        rows, lanes = x.shape
        lane = lax.broadcasted_iota(jnp.int32, x.shape, 1)
        row = lax.broadcasted_iota(jnp.int32, x.shape, 0)
        x = x + jnp.where(lane % 2 == 0, west(x), east(x))
        x = x + jnp.where(row % 2 == 0, up(x), down(x))
        out.append(0.25 * x)
    return tuple(out)


def mode_rate(step, modes):
    axis = modes.ndim - 2
    return (
        step[0] * modes
        + step[1] * pltpu.roll(modes, ROWS - 2, axis)
        + step[2] * pltpu.roll(modes, 4, axis)
        + step[3] * pltpu.roll(modes, 2, axis)
    )


def kernel(
    n, scanners,
    start_hbm, mob_hbm, left_hbm, right_hbm, back_right_hbm, back_left_hbm, step_hbm,
    out_ref,
    start_ref, mob_ref, left_ref, right_ref, back_right_ref, back_left_ref, step_ref, loaded,
    wide, fluct, arrived, modes, gathered, results, returned,
    w_send, w_recv, send_one, recv_one, send_two, recv_two,
):
    me = lax.axis_index("tm")
    grid = mob_ref.shape[-1]
    edge = (LANES - grid) // 2
    tiles = step_ref.shape[1]
    count = len(scanners)
    per = tiles // count
    MESH = pl.DeviceIdType.MESH

    loads = [
        pltpu.make_async_copy(src, dst, loaded.at[k])
        for k, (src, dst) in enumerate(
            [
                (start_hbm, start_ref),
                (mob_hbm, mob_ref),
                (left_hbm, left_ref),
                (right_hbm, right_ref),
                (step_hbm, step_ref),
                (back_right_hbm, back_right_ref),
                (back_left_hbm, back_left_ref),
            ]
        )
    ]
    for load in loads:
        load.start()
    barrier = pltpu.get_barrier_semaphore()

    def scans(index):
        hit = index == scanners[0]
        for d in scanners[1:]:
            hit = jnp.logical_or(hit, index == d)
        return hit

    one_of = scans(me)
    greeted = 0
    for d in range(n):
        if d in scanners:
            meets = me != d
        else:
            near = jnp.logical_or(me == d - 1, me == d + 1)
            meets = jnp.logical_or(near, one_of)
        greeted = greeted + jnp.where(meets, 1, 0)

        @pl.when(meets)
        def _():
            pl.semaphore_signal(barrier, inc=1, device_id={"tm": d}, device_id_type=MESH)

    lane = lax.broadcasted_iota(jnp.int32, (grid, LANES), 1)

    def widen(x, slot):
        wide[slot, :, :grid] = x
        x = wide[slot]
        return jnp.where(
            lane < grid,
            x,
            jnp.where(lane < grid + edge, pltpu.roll(x, grid, 1), pltpu.roll(x, 2 * edge, 1)),
        )

    loads[1].wait()
    mob = widen(mob_ref[0], 3)
    face_x = 0.5 * (mob + up(mob))
    face_y = 0.5 * (mob + west(mob))
    rate = lambda state: fine_rate(state, face_x, face_y)

    def forward(state):
        x = jnp.concatenate(state, axis=0)
        rows = tiles * ROWS
        g = product_left((left_ref[0], left_ref[1]), x)
        g = jnp.concatenate([g[:rows], g[rows:]], axis=1)
        return product_right(g, (right_ref[0], right_ref[1])).reshape(tiles, ROWS, LANES)

    def inverse(parts):
        rows = tiles * ROWS
        x = jnp.concatenate([p.reshape(rows, LANES) for p in parts], axis=0)
        z = product_right(x, (back_right_ref[0], back_right_ref[1]))
        z = jnp.concatenate(
            [
                jnp.concatenate([z[k * rows : (k + 1) * rows, s * LANES : (s + 1) * LANES] for k in range(len(parts))], axis=1)
                for s in range(2)
            ],
            axis=0,
        )
        y = product_left((back_left_ref[0], back_left_ref[1]), z)
        return [
            tuple(y[f * grid : (f + 1) * grid, k * LANES : (k + 1) * LANES] for f in range(3))
            for k in range(len(parts))
        ]

    def remote(src, dst, send, recv, target):
        return pltpu.make_async_remote_copy(
            src_ref=src, dst_ref=dst, send_sem=send, recv_sem=recv,
            device_id={"tm": target}, device_id_type=MESH,
        )

    def drain(ref, sem):
        pltpu.make_async_copy(ref, ref, sem).wait()

    def send(it, offsets):
        modes[it] = offsets
        for s, d in enumerate(scanners):
            @pl.when(me != d)
            def _():
                remote(
                    modes.at[it, pl.ds(s * per, per)], gathered.at[it, me],
                    send_one.at[it], recv_one.at[it], d,
                ).start()

    def scan(it, start_modes_ref, inclusive):
        for s, d in enumerate(scanners):
            @pl.when(me == d)
            def _():
                mine = [step_ref[k, s * per : (s + 1) * per] for k in range(4)]
                state = start_modes_ref[s * per : (s + 1) * per]
                gathered[it, d] = modes[it, s * per : (s + 1) * per]
                drain(gathered.at[it, pl.ds(0, n - 1)], recv_one.at[it])
                for k in range(n):
                    after = None
                    if inclusive or k + 1 < n:
                        after = state + (mode_rate(mine, state) + gathered[it, k])
                    value = after if inclusive else state
                    results[it, k] = value
                    if k == d:
                        returned[it, s * per : (s + 1) * per] = value
                    else:
                        remote(
                            results.at[it, k], returned.at[it, pl.ds(s * per, per)],
                            send_two.at[it], recv_two.at[it], k,
                        ).start()
                    state = after

    def scanned(it):
        @pl.when(one_of)
        def _():
            drain(returned.at[it, pl.ds(0, (count - 1) * per)], recv_two.at[it])

        @pl.when(jnp.logical_not(one_of))
        def _():
            drain(returned.at[it], recv_two.at[it])

        return returned[it]

    loads[0].wait()
    u0 = tuple(widen(start_ref[f], f) for f in range(3))
    f0 = rate(u0)
    u1 = combine((1.0, u0), (0.5 * DT, f0))
    a1 = rate(u1)
    w = combine((1.0, u1), (0.5 * DT, a1))
    pw = block_mean(w)
    wf = combine((1.0, w), (-1.0, pw))
    for f in range(3):
        fluct[f] = wf[f]
    for k in (2, 3, 4):
        loads[k].wait()
    step = [step_ref[k] for k in range(4)]
    start_modes = forward(u0)
    modes[2] = start_modes
    a2 = rate(w)
    integral = combine((DT / 6.0, f0), (DT * 2.0 / 3.0, a1), (DT / 6.0, a2))
    offsets = forward(integral) - mode_rate(step, start_modes)
    pl.semaphore_wait(barrier, greeted)
    send(0, offsets)

    @pl.when(me + 1 < n)
    def _():
        remote(fluct, arrived, w_send, w_recv, me + 1).start()

    scan(0, modes.at[2], False)

    p0 = block_mean(u0)
    u1f = combine((1.0, u1), (-0.5, p0), (-0.5, pw))

    @pl.when(me == 0)
    def _():
        for f in range(3):
            arrived[f] = u0[f] - p0[f]

    for k in (5, 6):
        loads[k].wait()
    begin = scanned(0)
    end = begin + (mode_rate(step, begin) + offsets)
    pb, pe = inverse([begin, end])

    @pl.when(me > 0)
    def _():
        drain(arrived, w_recv)

    u0 = tuple(arrived[f] + pb[f] for f in range(3))
    u1 = combine((1.0, u1f), (0.5, pb), (0.5, pe))
    u2 = combine((1.0, wf), (1.0, pe))
    f1 = rate(u1)
    f2 = rate(u2)
    a0 = rate(u0)
    u1 = combine(
        (1.0, u0), (0.5 * DT, a0), (DT * (5.0 / 24.0 - 0.5), f0), (DT / 3.0, f1), (-DT / 24.0, f2)
    )
    a1 = rate(u1)
    w = combine(
        (1.0, u1), (0.5 * DT, a1), (-DT / 24.0, f0), (DT * (1.0 / 3.0 - 0.5), f1), (DT * 5.0 / 24.0, f2)
    )
    a2 = rate(w)
    integral = combine((DT / 6.0, a0), (DT * 2.0 / 3.0, a1), (DT / 6.0, a2))
    offsets = forward(integral) - mode_rate(step, begin)
    send(1, offsets)
    scan(1, modes.at[2], True)
    pw = block_mean(w)
    wf = combine((1.0, w), (-1.0, pw))
    for f in range(3):
        wide[f] = wf[f]
    (pe,) = inverse([scanned(1)])
    for f in range(3):
        out_ref[0, f] = (wide[f] + pe[f])[:, :grid]

    @pl.when(me + 1 < n)
    def _():
        drain(fluct, w_send)

    for it in range(2):
        @pl.when(one_of)
        def _():
            drain(modes.at[it, pl.ds(0, (count - 1) * per)], send_one.at[it])
            drain(results.at[it, pl.ds(0, n - 1)], send_two.at[it])

        @pl.when(jnp.logical_not(one_of))
        def _():
            drain(modes.at[it], send_one.at[it])


def local(n, start_state, mobility):
    grid = start_state.shape[-1]
    made = constants(grid)
    tiles = made[-1].shape[1]
    count = tiles // PER
    first, width = (n // 4, n // 2) if n // 2 >= count else (0, n)
    scanners = tuple(first + s * width // count for s in range(count))
    return pl.pallas_call(
        functools.partial(kernel, n, scanners),
        out_shape=jax.ShapeDtypeStruct((1,) + start_state.shape, F32),
        in_specs=[pl.BlockSpec(memory_space=pl.ANY)] * (2 + len(made)),
        out_specs=pl.BlockSpec(memory_space=pltpu.VMEM),
        scratch_shapes=[pltpu.VMEM(x.shape, x.dtype) for x in (start_state, mobility, *made)]
        + [
            pltpu.SemaphoreType.DMA((2 + len(made),)),
            pltpu.VMEM((4, grid, LANES), F32),
            pltpu.VMEM((3, grid, LANES), F32),
            pltpu.VMEM((3, grid, LANES), F32),
            pltpu.VMEM((3, tiles, ROWS, LANES), F32),
            pltpu.VMEM((2, n, PER, ROWS, LANES), F32),
            pltpu.VMEM((2, n, PER, ROWS, LANES), F32),
            pltpu.VMEM((2, tiles, ROWS, LANES), F32),
            pltpu.SemaphoreType.DMA,
            pltpu.SemaphoreType.DMA,
            pltpu.SemaphoreType.DMA((2,)),
            pltpu.SemaphoreType.DMA((2,)),
            pltpu.SemaphoreType.DMA((2,)),
            pltpu.SemaphoreType.DMA((2,)),
        ],
        compiler_params=pltpu.CompilerParams(
            collective_id=0, has_side_effects=True, vmem_limit_bytes=60 * 1024 * 1024
        ),
        cost_estimate=pl.CostEstimate(flops=200_000_000, bytes_accessed=1_500_000, transcendentals=0),
    )(start_state, mobility, *[jnp.asarray(m) for m in made])


def solution(mesh):
    n = mesh.shape["tm"]
    in_specs = (P("groups", None, None), P("tm", "groups", None))
    out_specs = P("tm", "groups", None, None)
    return jax.shard_map(
        functools.partial(local, n), mesh=mesh, in_specs=in_specs, out_specs=out_specs, check_vma=False
    )
```

```python
import functools

import jax
import jax.numpy as jnp
import ml_dtypes
import numpy as np
from jax import lax
from jax.experimental import pallas as pl
from jax.experimental.pallas import tpu as pltpu
from jax.sharding import PartitionSpec as P

DT = 0.015
KAPPA = 1.0
ETA = 0.5
DE = 0.5
GAMMA = 2.0
M1 = 0.6
M2 = -0.4
MEAN = 1.0
LANES = 128
ROWS = 8
PER = 2
F32 = jnp.float32
BF16 = jnp.bfloat16


def split(matrix):
    high = matrix.astype(ml_dtypes.bfloat16)
    low = (matrix - high.astype(np.float64)).astype(ml_dtypes.bfloat16)
    return high, low


def constants(grid):
    half = grid // 2
    tiles = half // 4
    rows = tiles * ROWS
    wave = np.arange(half)
    angle = 2.0 * np.pi * np.outer(wave, wave) / half
    basis = (np.cos(angle) + np.sin(angle)) / np.sqrt(half)
    mean = 0.5 * np.repeat(basis, 2, axis=1)
    spread = np.repeat(basis, 2, axis=0)
    edge = (LANES - grid) // 2
    lane = np.arange(LANES)
    column = np.where(lane < grid, lane, np.where(lane < grid + edge, lane - grid, lane - 2 * edge))
    left = np.zeros((2 * rows, 3 * grid))
    right = np.zeros((2 * LANES, LANES))
    back_right = np.zeros((LANES, 2 * LANES))
    back_left = np.zeros((3 * grid, 2 * rows))
    square = np.sin(np.pi * wave / half) ** 2
    step = np.zeros((4, rows, LANES))
    for s in range(2):
        right[s * LANES : s * LANES + grid, s * half : (s + 1) * half] = mean.T
        back_right[s * half : (s + 1) * half, s * LANES : (s + 1) * LANES] = spread[column].T
        lanes = slice(s * half, (s + 1) * half)
        for j in range(tiles):
            for h in range(2):
                a = 4 * j + 2 * h + s
                sym = -(square[a] + square)
                for f in range(3):
                    row = ROWS * j + 2 * f + h
                    left[s * rows + row, f * grid : (f + 1) * grid] = mean[a]
                    back_left[f * grid : (f + 1) * grid, s * rows + row] = spread[:, a]
                row = ROWS * j + h
                step[0, row, lanes] = MEAN * (-sym - KAPPA * sym * sym)
                step[1, row, lanes] = MEAN * ETA * sym
                step[2, row, lanes] = MEAN * ETA * sym
                step[0, row + 2, lanes] = DE * sym - GAMMA
                step[0, row + 4, lanes] = DE * sym - GAMMA
                step[3, row + 2, lanes] = GAMMA * M1
                step[2, row + 4, lanes] = GAMMA * M2
    step = (DT * step).astype(np.float32).reshape(4, tiles, ROWS, LANES)
    return [np.stack(split(matrix)) for matrix in (left, right, back_right, back_left)] + [step]


def product_left(pair, x):
    high_c, low_c = pair
    high = x.astype(BF16)
    low = (x - high.astype(F32)).astype(BF16)
    dot = functools.partial(jnp.dot, preferred_element_type=F32)
    return dot(high_c, high) + (dot(high_c, low) + dot(low_c, high))


def product_right(x, pair):
    high_c, low_c = pair
    high = x.astype(BF16)
    low = (x - high.astype(F32)).astype(BF16)
    dot = functools.partial(jnp.dot, preferred_element_type=F32)
    return dot(high, high_c) + (dot(low, high_c) + dot(high, low_c))


def up(x):
    return pltpu.roll(x, x.shape[0] - 1, 0)


def down(x):
    return pltpu.roll(x, 1, 0)


def west(x):
    return pltpu.roll(x, LANES - 1, 1)


def east(x):
    return pltpu.roll(x, 1, 1)


def laplace(x):
    return (up(x) + down(x)) + (west(x) + east(x)) - 4.0 * x


def fine_rate(state, face_x, face_y):
    c, one, two = state
    mu = c * c * c - c - KAPPA * laplace(c) + ETA * (one + two)
    jx = face_x * (up(mu) - mu)
    jy = face_y * (west(mu) - mu)
    rate_c = (jx - down(jx)) + (jy - east(jy))
    rate_one = DE * laplace(one) - GAMMA * (one - M1 * c)
    rate_two = DE * laplace(two) - GAMMA * (two - M2 * c)
    return rate_c, rate_one, rate_two


def combine(*terms):
    total = None
    for weight, state in terms:
        part = state if weight == 1.0 else tuple(weight * x for x in state)
        total = part if total is None else tuple(a + b for a, b in zip(total, part))
    return total


def block_mean(state):
    out = []
    for x in state:
        rows, lanes = x.shape
        lane = lax.broadcasted_iota(jnp.int32, x.shape, 1)
        row = lax.broadcasted_iota(jnp.int32, x.shape, 0)
        x = x + jnp.where(lane % 2 == 0, west(x), east(x))
        x = x + jnp.where(row % 2 == 0, up(x), down(x))
        out.append(0.25 * x)
    return tuple(out)


def mode_rate(step, modes):
    axis = modes.ndim - 2
    return (
        step[0] * modes
        + step[1] * pltpu.roll(modes, ROWS - 2, axis)
        + step[2] * pltpu.roll(modes, 4, axis)
        + step[3] * pltpu.roll(modes, 2, axis)
    )


def kernel(
    n, scanners,
    start_hbm, mob_hbm, left_hbm, right_hbm, back_right_hbm, back_left_hbm, step_hbm,
    out_ref,
    start_ref, mob_ref, left_ref, right_ref, back_right_ref, back_left_ref, step_ref, loaded,
    wide, fluct, arrived, modes, gathered, results, returned,
    w_send, w_recv, send_one, recv_one, send_two, recv_two,
):
    me = lax.axis_index("tm")
    grid = mob_ref.shape[-1]
    edge = (LANES - grid) // 2
    tiles = step_ref.shape[1]
    count = len(scanners)
    per = tiles // count
    MESH = pl.DeviceIdType.MESH

    loads = [
        pltpu.make_async_copy(src, dst, loaded.at[k])
        for k, (src, dst) in enumerate(
            [
                (start_hbm, start_ref),
                (mob_hbm, mob_ref),
                (left_hbm, left_ref),
                (right_hbm, right_ref),
                (step_hbm, step_ref),
                (back_right_hbm, back_right_ref),
                (back_left_hbm, back_left_ref),
            ]
        )
    ]
    for load in loads:
        load.start()
    barrier = pltpu.get_barrier_semaphore()

    def scans(index):
        hit = index == scanners[0]
        for d in scanners[1:]:
            hit = jnp.logical_or(hit, index == d)
        return hit

    one_of = scans(me)
    greeted = 0
    for d in range(n):
        if d in scanners:
            meets = me != d
        else:
            near = jnp.logical_or(me == d - 1, me == d + 1)
            meets = jnp.logical_or(near, one_of)
        greeted = greeted + jnp.where(meets, 1, 0)

        @pl.when(meets)
        def _():
            pl.semaphore_signal(barrier, inc=1, device_id={"tm": d}, device_id_type=MESH)

    lane = lax.broadcasted_iota(jnp.int32, (grid, LANES), 1)

    def widen(x, slot):
        wide[slot, :, :grid] = x
        x = wide[slot]
        return jnp.where(
            lane < grid,
            x,
            jnp.where(lane < grid + edge, pltpu.roll(x, grid, 1), pltpu.roll(x, 2 * edge, 1)),
        )

    loads[1].wait()
    mob = widen(mob_ref[0], 3)
    face_x = 0.5 * (mob + up(mob))
    face_y = 0.5 * (mob + west(mob))
    rate = lambda state: fine_rate(state, face_x, face_y)

    def forward(state):
        x = jnp.concatenate(state, axis=0)
        rows = tiles * ROWS
        g = product_left((left_ref[0], left_ref[1]), x)
        g = jnp.concatenate([g[:rows], g[rows:]], axis=1)
        return product_right(g, (right_ref[0], right_ref[1])).reshape(tiles, ROWS, LANES)

    def inverse(parts):
        rows = tiles * ROWS
        x = jnp.concatenate([p.reshape(rows, LANES) for p in parts], axis=0)
        z = product_right(x, (back_right_ref[0], back_right_ref[1]))
        z = jnp.concatenate(
            [
                jnp.concatenate([z[k * rows : (k + 1) * rows, s * LANES : (s + 1) * LANES] for k in range(len(parts))], axis=1)
                for s in range(2)
            ],
            axis=0,
        )
        y = product_left((back_left_ref[0], back_left_ref[1]), z)
        return [
            tuple(y[f * grid : (f + 1) * grid, k * LANES : (k + 1) * LANES] for f in range(3))
            for k in range(len(parts))
        ]

    def remote(src, dst, send, recv, target):
        return pltpu.make_async_remote_copy(
            src_ref=src, dst_ref=dst, send_sem=send, recv_sem=recv,
            device_id={"tm": target}, device_id_type=MESH,
        )

    def drain(ref, sem):
        pltpu.make_async_copy(ref, ref, sem).wait()

    def send(it, offsets):
        modes[it] = offsets
        for s, d in enumerate(scanners):
            @pl.when(me != d)
            def _():
                remote(
                    modes.at[it, pl.ds(s * per, per)], gathered.at[it, me],
                    send_one.at[it], recv_one.at[it], d,
                ).start()

    def scan(it, start_modes_ref, inclusive):
        for s, d in enumerate(scanners):
            @pl.when(me == d)
            def _():
                mine = [step_ref[k, s * per : (s + 1) * per] for k in range(4)]
                state = start_modes_ref[s * per : (s + 1) * per]
                gathered[it, d] = modes[it, s * per : (s + 1) * per]
                drain(gathered.at[it, pl.ds(0, n - 1)], recv_one.at[it])
                for k in range(n):
                    after = None
                    if inclusive or k + 1 < n:
                        after = state + (mode_rate(mine, state) + gathered[it, k])
                    value = after if inclusive else state
                    results[it, k] = value
                    if k == d:
                        returned[it, s * per : (s + 1) * per] = value
                    else:
                        remote(
                            results.at[it, k], returned.at[it, pl.ds(s * per, per)],
                            send_two.at[it], recv_two.at[it], k,
                        ).start()
                    state = after

    def scanned(it):
        @pl.when(one_of)
        def _():
            drain(returned.at[it, pl.ds(0, (count - 1) * per)], recv_two.at[it])

        @pl.when(jnp.logical_not(one_of))
        def _():
            drain(returned.at[it], recv_two.at[it])

        return returned[it]

    loads[0].wait()
    u0 = tuple(widen(start_ref[f], f) for f in range(3))
    f0 = rate(u0)
    u1 = combine((1.0, u0), (0.5 * DT, f0))
    a1 = rate(u1)
    w = combine((1.0, u1), (0.5 * DT, a1))
    pw = block_mean(w)
    wf = combine((1.0, w), (-1.0, pw))
    for f in range(3):
        fluct[f] = wf[f]
    for k in (2, 3, 4):
        loads[k].wait()
    step = [step_ref[k] for k in range(4)]
    start_modes = forward(u0)
    modes[2] = start_modes
    a2 = rate(w)
    integral = combine((DT / 6.0, f0), (DT * 2.0 / 3.0, a1), (DT / 6.0, a2))
    offsets = forward(integral) - mode_rate(step, start_modes)
    pl.semaphore_wait(barrier, greeted)
    send(0, offsets)

    @pl.when(me + 1 < n)
    def _():
        remote(fluct, arrived, w_send, w_recv, me + 1).start()

    scan(0, modes.at[2], False)

    p0 = block_mean(u0)
    u1f = combine((1.0, u1), (-0.5, p0), (-0.5, pw))

    @pl.when(me == 0)
    def _():
        for f in range(3):
            arrived[f] = u0[f] - p0[f]

    for k in (5, 6):
        loads[k].wait()
    begin = scanned(0)
    end = begin + (mode_rate(step, begin) + offsets)
    pb, pe = inverse([begin, end])

    @pl.when(me > 0)
    def _():
        drain(arrived, w_recv)

    u0 = tuple(arrived[f] + pb[f] for f in range(3))
    u1 = combine((1.0, u1f), (0.5, pb), (0.5, pe))
    u2 = combine((1.0, wf), (1.0, pe))
    f1 = rate(u1)
    f2 = rate(u2)
    a0 = rate(u0)
    u1 = combine(
        (1.0, u0), (0.5 * DT, a0), (DT * (5.0 / 24.0 - 0.5), f0), (DT / 3.0, f1), (-DT / 24.0, f2)
    )
    a1 = rate(u1)
    w = combine(
        (1.0, u1), (0.5 * DT, a1), (-DT / 24.0, f0), (DT * (1.0 / 3.0 - 0.5), f1), (DT * 5.0 / 24.0, f2)
    )
    a2 = rate(w)
    integral = combine((DT / 6.0, a0), (DT * 2.0 / 3.0, a1), (DT / 6.0, a2))
    offsets = forward(integral) - mode_rate(step, begin)
    send(1, offsets)
    scan(1, modes.at[2], True)
    pw = block_mean(w)
    wf = combine((1.0, w), (-1.0, pw))
    for f in range(3):
        wide[f] = wf[f]
    (pe,) = inverse([scanned(1)])
    for f in range(3):
        out_ref[0, f] = (wide[f] + pe[f])[:, :grid]

    @pl.when(me + 1 < n)
    def _():
        drain(fluct, w_send)

    for it in range(2):
        @pl.when(one_of)
        def _():
            drain(modes.at[it, pl.ds(0, (count - 1) * per)], send_one.at[it])
            drain(results.at[it, pl.ds(0, n - 1)], send_two.at[it])

        @pl.when(jnp.logical_not(one_of))
        def _():
            drain(modes.at[it], send_one.at[it])


def local(n, start_state, mobility):
    grid = start_state.shape[-1]
    made = constants(grid)
    tiles = made[-1].shape[1]
    count = tiles // PER
    first, width = (n // 4, n // 2) if n // 2 >= count else (0, n)
    scanners = tuple(first + s * width // count for s in range(count))
    return pl.pallas_call(
        functools.partial(kernel, n, scanners),
        out_shape=pltpu.VMEM((1,) + start_state.shape, F32),
        in_specs=[pl.BlockSpec(memory_space=pl.ANY)] * (2 + len(made)),
        out_specs=pl.BlockSpec(memory_space=pltpu.VMEM),
        scratch_shapes=[pltpu.VMEM(x.shape, x.dtype) for x in (start_state, mobility, *made)]
        + [
            pltpu.SemaphoreType.DMA((2 + len(made),)),
            pltpu.VMEM((4, grid, LANES), F32),
            pltpu.VMEM((3, grid, LANES), F32),
            pltpu.VMEM((3, grid, LANES), F32),
            pltpu.VMEM((3, tiles, ROWS, LANES), F32),
            pltpu.VMEM((2, n, PER, ROWS, LANES), F32),
            pltpu.VMEM((2, n, PER, ROWS, LANES), F32),
            pltpu.VMEM((2, tiles, ROWS, LANES), F32),
            pltpu.SemaphoreType.DMA,
            pltpu.SemaphoreType.DMA,
            pltpu.SemaphoreType.DMA((2,)),
            pltpu.SemaphoreType.DMA((2,)),
            pltpu.SemaphoreType.DMA((2,)),
            pltpu.SemaphoreType.DMA((2,)),
        ],
        compiler_params=pltpu.CompilerParams(
            collective_id=0, has_side_effects=True, vmem_limit_bytes=56 * 1024 * 1024
        ),
        cost_estimate=pl.CostEstimate(flops=200_000_000, bytes_accessed=1_500_000, transcendentals=0),
    )(start_state, mobility, *[jnp.asarray(m) for m in made])


def solution(mesh):
    n = mesh.shape["tm"]
    in_specs = (P("groups", None, None), P("tm", "groups", None))
    out_specs = P("tm", "groups", None, None)
    return jax.shard_map(
        functools.partial(local, n), mesh=mesh, in_specs=in_specs, out_specs=out_specs, check_vma=False
    )
```
